128 devices in a mesh: rollout: 16 (over y, x_hi, core), tp: 8 (over z, x_lo).
Axes of the slice: x: 4 (x_hi: 2, x_lo: 2; x = x_hi * 2 + x_lo), y: 4, z: 4, core: 2. Of those that a mesh axis runs over, the one named last changes fastest.
Arguments:
- tokens: bfloat16 [4096, 8192], P('rollout'), may hold values from -800 to 800
- norm_gain: float32 [8192], replicated, may hold values from 0.5 to 1.5
- query_weight: bfloat16 [8192, 8192], P(None, 'tp'), may hold values from -0.0625 to 0.0625
- key_matrix: bfloat16 [8192, 1024], P(None, 'tp'), may hold values from -0.25 to 0.25
- value_matrix: bfloat16 [8192, 1024], P(None, 'tp'), may hold values from -0.0625 to 0.0625
- prompt_cache: bfloat16 [2, 16384, 8, 128], P(None, ('rollout', 'tp')), may hold values from -330 to 330
- lengths: int32 [16], P('rollout'), may hold values from 128 to 256, as said below
Outputs:
- context: bfloat16 [4096, 8192], P('rollout', 'tp')
The draws below stay inside these ranges and needn't reach their ends.
Inputs may be any that keep to these rules, and one draw needn't show every extreme that they name: `lengths`: each length is a multiple of 128.
All inputs are finite; a program needn't handle non-finite values.
Results may differ from the reference program's by a relative error of at most 0.022.
Values may be sent and summed in bfloat16 or wider, within the bound.
A program may use at most 320 MiB of HBM per device.

```python
import math
import jax
import jax.numpy as jnp
from jax import lax

MODEL_WIDTH = 8192
QUERY_HEADS = 64
KEY_VALUE_HEADS = 8
HEAD_SIZE = 128
COMPLETION_SLOTS = 256
BLOCK = 128
SAMPLE_TOTAL = 16
PROMPT_TOTAL = 16384


def draw_tokens(key, part):
    key = jax.random.fold_in(key, 1)
    key_scale, key_base = jax.random.split(key, 2)
    count_of_rows = SAMPLE_TOTAL * COMPLETION_SLOTS
    column_scale = jnp.exp(jax.random.uniform(key_scale, (1, MODEL_WIDTH), jnp.float32, 0.0, math.log(10.0)))
    values = jnp.clip(jax.random.normal(key_base, (count_of_rows, MODEL_WIDTH), jnp.float32), -6.0, 6.0) * column_scale
    return values.astype(jnp.bfloat16)


def draw_prompt_cache(key, part):
    key = jax.random.fold_in(key, 2)
    key_keys, key_values = jax.random.split(key, 2)
    array_shape = (PROMPT_TOTAL, KEY_VALUE_HEADS, HEAD_SIZE)
    key_part = jnp.clip(jax.random.normal(key_keys, array_shape, jnp.float32), -6.0, 6.0) * 3.0
    value_part = jnp.clip(jax.random.normal(key_values, array_shape, jnp.float32), -6.0, 6.0)
    return jnp.stack([key_part, value_part]).astype(jnp.bfloat16)


def draw_lengths(key, part):
    key = jax.random.fold_in(key, 3)
    key_blocks, key_pick = jax.random.split(key)
    most_blocks = COMPLETION_SLOTS // BLOCK
    blocks = jax.random.randint(key_blocks, (SAMPLE_TOTAL,), 1, most_blocks + 1)
    chosen = jax.random.randint(key_pick, (), 0, SAMPLE_TOTAL)
    blocks = jnp.where(jnp.arange(SAMPLE_TOTAL) == chosen, most_blocks, blocks)
    return (blocks * BLOCK).astype(jnp.int32)


def levels(stream_key, extent, cuts, smallest, high):
    level, own = 1.0, jax.random.fold_in(stream_key, 6)
    for axis_at, shards_of in cuts:
        heights = jnp.exp(jax.random.uniform(jax.random.fold_in(own, axis_at), (shards_of,), jnp.float32, smallest / len(cuts), high / len(cuts)))
        level = level * jnp.repeat(heights, extent[axis_at] // shards_of).reshape([-1 if axis == axis_at else 1 for axis in range(len(extent))])
    return level


def centred(own_key, extent, width, reach, shards=(), kind=jnp.bfloat16):
    level = levels(own_key, extent, shards, -0.22, 0.18) if shards else 1.0
    drawn = jax.random.normal(own_key, extent, jnp.float32) * width * level
    return jnp.minimum(jnp.maximum(drawn, -reach), reach).astype(kind)


def setup_inputs(seed: int = 0) -> dict:
    keys = jax.random.split(jax.random.key(seed), 8)
    tokens = draw_tokens(jax.random.fold_in(keys[7], 71), 0)
    norm_gain = jnp.clip(1.0 + 0.1 * jax.random.normal(keys[1], (MODEL_WIDTH,), jnp.float32), 0.5, 1.5)
    query_weight = centred(keys[2], (MODEL_WIDTH, QUERY_HEADS * HEAD_SIZE), MODEL_WIDTH ** -0.5, 0.0625, ((1, 8),))
    key_matrix = centred(keys[3], (MODEL_WIDTH, KEY_VALUE_HEADS * HEAD_SIZE), (MODEL_WIDTH // 16) ** -0.5, 0.25, ((1, 8),))
    value_matrix = centred(keys[4], (MODEL_WIDTH, KEY_VALUE_HEADS * HEAD_SIZE), MODEL_WIDTH ** -0.5, 0.0625, ((1, 8),))
    prompt_cache = draw_prompt_cache(jax.random.fold_in(keys[7], 71), 0)
    lengths = draw_lengths(jax.random.fold_in(keys[7], 71), 0)
    return {"tokens": tokens, "norm_gain": norm_gain, "query_weight": query_weight, "key_matrix": key_matrix, "value_matrix": value_matrix, "prompt_cache": prompt_cache, "lengths": lengths}


rope_base = 500000.0

def rotary_apply(values, token_position):
    half_width = values.shape[-1] // 2
    frequency = jnp.power(jnp.float32(rope_base), -2.0 * jnp.arange(half_width, dtype=jnp.float32) / values.shape[-1])
    angles = token_position[:, None] * frequency[None, :]
    cos_shape = (values.shape[0],) + (1,) * (values.ndim - 2) + (half_width,)
    cosine = jnp.cos(angles).reshape(cos_shape)
    sine_part = jnp.sin(angles).reshape(cos_shape)
    lower_half = values[..., :half_width]
    upper_half = values[..., half_width:]
    return jnp.concatenate([lower_half * cosine - upper_half * sine_part, upper_half * cosine + lower_half * sine_part], axis=-1)

def reference(tokens, norm_gain, query_weight, key_matrix, value_matrix, prompt_cache, lengths):
    count_of_rows = SAMPLE_TOTAL * COMPLETION_SLOTS
    query_group_size = QUERY_HEADS // KEY_VALUE_HEADS
    score_scale = HEAD_SIZE ** (-0.5)
    widened = tokens.astype(jnp.float32)
    normalized_input = (widened * lax.rsqrt(lax.optimization_barrier(jnp.mean(widened * widened, axis=-1, keepdims=True)) + 1e-05) * norm_gain).astype(jnp.bfloat16)
    token_position = (PROMPT_TOTAL + jnp.arange(count_of_rows) % COMPLETION_SLOTS).astype(jnp.float32)
    query_matrix = rotary_apply(jnp.dot(normalized_input, query_weight, preferred_element_type=jnp.float32).reshape(count_of_rows, QUERY_HEADS, HEAD_SIZE), token_position).astype(jnp.bfloat16)
    fresh_key = rotary_apply(jnp.dot(normalized_input, key_matrix, preferred_element_type=jnp.float32).reshape(count_of_rows, KEY_VALUE_HEADS, HEAD_SIZE), token_position).astype(jnp.bfloat16)
    fresh_value = jnp.dot(normalized_input, value_matrix, preferred_element_type=jnp.float32).astype(jnp.bfloat16).reshape(count_of_rows, KEY_VALUE_HEADS, HEAD_SIZE)
    query_matrix = query_matrix.reshape(SAMPLE_TOTAL, COMPLETION_SLOTS, KEY_VALUE_HEADS, query_group_size, HEAD_SIZE).transpose(0, 2, 1, 3, 4).reshape(SAMPLE_TOTAL * KEY_VALUE_HEADS, COMPLETION_SLOTS, query_group_size, HEAD_SIZE)
    fresh_key = fresh_key.reshape(SAMPLE_TOTAL, COMPLETION_SLOTS, KEY_VALUE_HEADS, HEAD_SIZE).transpose(0, 2, 1, 3).reshape(SAMPLE_TOTAL * KEY_VALUE_HEADS, COMPLETION_SLOTS, HEAD_SIZE)
    fresh_value = fresh_value.reshape(SAMPLE_TOTAL, COMPLETION_SLOTS, KEY_VALUE_HEADS, HEAD_SIZE).transpose(0, 2, 1, 3).reshape(SAMPLE_TOTAL * KEY_VALUE_HEADS, COMPLETION_SLOTS, HEAD_SIZE)
    causal = jnp.arange(COMPLETION_SLOTS)[None, :] <= jnp.arange(COMPLETION_SLOTS)[:, None]

    def attend_prompt(flattened_index):
        sample_index = flattened_index // KEY_VALUE_HEADS
        key_value_head = flattened_index % KEY_VALUE_HEADS
        query_rows = query_matrix[flattened_index].astype(jnp.float32)
        prompt_keys = prompt_cache[0, :, key_value_head].astype(jnp.float32)
        prompt_values = prompt_cache[1, :, key_value_head].astype(jnp.float32)
        own_keys = fresh_key[flattened_index].astype(jnp.float32)
        own_values = fresh_value[flattened_index].astype(jnp.float32)
        far_scores = jnp.einsum('tqd,pd->tqp', query_rows, prompt_keys) * score_scale
        near_scores = jnp.einsum('tqd,ud->tqu', query_rows, own_keys) * score_scale
        near_scores = jnp.where(causal[:, None, :], near_scores, -jnp.inf)
        row_top = jnp.maximum(far_scores.max(axis=-1), near_scores.max(axis=-1))
        far_weights = jnp.exp(far_scores - row_top[..., None])
        near_weights = jnp.exp(near_scores - row_top[..., None])
        row_total = far_weights.sum(axis=-1) + near_weights.sum(axis=-1)
        far_rounded = lax.optimization_barrier(far_weights.astype(jnp.bfloat16)).astype(jnp.float32)
        near_rounded = lax.optimization_barrier(near_weights.astype(jnp.bfloat16)).astype(jnp.float32)
        blended = jnp.einsum('tqp,pd->tqd', far_rounded, prompt_values) + jnp.einsum('tqu,ud->tqd', near_rounded, own_values)
        result = blended / row_total[..., None]
        live_rows = jnp.arange(COMPLETION_SLOTS) < lengths[sample_index]
        return jnp.where(live_rows[:, None, None], result, 0.0).astype(jnp.bfloat16)
    stacked_rows = lax.map(attend_prompt, jnp.arange(SAMPLE_TOTAL * KEY_VALUE_HEADS))
    return stacked_rows.reshape(SAMPLE_TOTAL, KEY_VALUE_HEADS, COMPLETION_SLOTS, query_group_size, HEAD_SIZE).transpose(0, 2, 1, 3, 4).reshape(count_of_rows, QUERY_HEADS * HEAD_SIZE)
```

```python
import functools

import jax
import jax.numpy as jnp
import numpy as np
from jax import lax
from jax.experimental import pallas as pl
from jax.experimental.pallas import tpu as pltpu
from jax.sharding import PartitionSpec as P

F32, BF16 = jnp.float32, jnp.bfloat16
MESH = pl.DeviceIdType.MESH
HEAD = 128
ROWS = 256
GROUP = 8
WIDTH = 8192
PARTS = 8
PART = WIDTH // PARTS
TP, ROLLOUT = 8, 16
PIECE = 128
CHUNK = PIECE * TP
PROMPT = CHUNK * ROLLOUT
ROPE_BASE = 500000.0
SCALE = float(HEAD ** -0.5 * np.log2(np.e))

OWN, SIB_OWN, UP, DOWN, SIB_UP, SIB_DOWN, ACROSS, SIB_ACROSS = range(8)
FAR, SIB_FAR, UP_A, DOWN_A, SIB_UP_A, SIB_DOWN_A, FAR_A, SIB_FAR_A = range(8, 16)


def tables():
    half = HEAD // 2
    frequency = np.power(
        np.float32(ROPE_BASE), -2.0 * np.arange(half, dtype=np.float32) / np.float32(HEAD)
    ).astype(np.float32)
    position = (PROMPT + np.arange(ROWS)).astype(np.float32)
    angles = (position[:, None] * frequency[None, :]).astype(np.float32).astype(np.float64)
    cosine, sine = np.cos(angles), np.sin(angles)
    return (
        np.concatenate([cosine, cosine], axis=1).astype(np.float32),
        np.concatenate([-sine, sine], axis=1).astype(np.float32),
    )


def kernel(
    tokens, gain, wq, wk, wv, cache, length, cos_ref, sin_ref, out,
    tok, normed, wq_v, wk_v, wv_v, proj, kv, q, fresh, top, acc,
    tok_sem, w_sem, own_sem, a_send, a_recv, send, recv,
):
    r, t = lax.axis_index("rollout"), lax.axis_index("tp")
    y, low = r // 4, r % 4
    core, across = r % 2, (r // 2) % 2
    sibling = r + 1 - 2 * core
    partner = r + 2 - 4 * across
    up = ((y + 1) % 4) * 4 + low
    down = ((y + 3) % 4) * 4 + low
    half = CHUNK // 2

    def tok_copy(i):
        return pltpu.make_async_copy(
            tokens.at[:, pl.ds(pl.multiple_of(i * PART, PART), PART)], tok.at[i], tok_sem.at[i]
        )

    def w_copies(i):
        rows = pl.ds(pl.multiple_of(i * PART, PART), PART)
        return [
            pltpu.make_async_copy(wq.at[rows], wq_v.at[i], w_sem.at[0, i]),
            pltpu.make_async_copy(wk.at[rows], wk_v.at[i], w_sem.at[1, i]),
            pltpu.make_async_copy(wv.at[rows], wv_v.at[i], w_sem.at[2, i]),
        ]

    def start_loads(i, _):
        tok_copy(i).start()
        return 0

    def start_weights(i, _):
        for c in w_copies(i):
            c.start()
        return 0

    lax.fori_loop(0, PARTS, start_loads, 0)
    lax.fori_loop(0, PARTS, start_weights, 0)

    barrier = pltpu.get_barrier_semaphore()
    for d in range(1, TP):
        pl.semaphore_signal(barrier, inc=1, device_id=(r, (t + d) % TP), device_id_type=MESH)
    for other in (sibling, partner, up, down):
        pl.semaphore_signal(barrier, inc=1, device_id=(other, t), device_id_type=MESH)
    pl.semaphore_wait(barrier, TP - 1 + 4)

    def a_copy(d):
        head = (t + d) % TP
        return pltpu.make_async_remote_copy(
            src_ref=cache.at[head],
            dst_ref=kv.at[OWN, :, pl.ds(pl.multiple_of(t * PIECE, PIECE), PIECE)],
            send_sem=a_send.at[d - 1], recv_sem=a_recv.at[d - 1],
            device_id=(r, head), device_id_type=MESH,
        )

    def a_arrival(d):
        source = (t + TP - d) % TP
        return pltpu.make_async_remote_copy(
            src_ref=cache.at[t],
            dst_ref=kv.at[OWN, :, pl.ds(pl.multiple_of(source * PIECE, PIECE), PIECE)],
            send_sem=a_send.at[d - 1], recv_sem=a_recv.at[d - 1],
            device_id=(r, t), device_id_type=MESH,
        )

    own = pltpu.make_async_copy(
        cache.at[t], kv.at[OWN, :, pl.ds(pl.multiple_of(t * PIECE, PIECE), PIECE)], own_sem
    )
    for d in range(1, TP):
        a_copy(d).start()
    own.start()

    moves = {}

    def move(name, source, target, device, rows=None):
        index = len(moves)
        if rows is None:
            src, dst = kv.at[source], kv.at[target]
        else:
            src, dst = kv.at[source, :, rows], kv.at[target, :, rows]
        moves[name] = pltpu.make_async_remote_copy(
            src_ref=src, dst_ref=dst, send_sem=send.at[index], recv_sem=recv.at[index],
            device_id=(device, t), device_id_type=MESH,
        )

    first, second = pl.ds(0, half), pl.ds(half, half)
    move("own_across", OWN, ACROSS, partner)
    move("own_up", OWN, UP, up)
    move("own_down", OWN, DOWN, down)
    move("sib_own", OWN, SIB_OWN, sibling)
    move("sib_up", UP, SIB_UP, sibling)
    move("sib_down", DOWN, SIB_DOWN, sibling)
    move("far_up", UP, FAR, up, first)
    move("far_down", DOWN, FAR, down, second)
    move("sib_across", ACROSS, SIB_ACROSS, sibling)
    move("across_up", ACROSS, UP_A, up)
    move("across_down", ACROSS, DOWN_A, down)
    move("sib_far", FAR, SIB_FAR, sibling)
    move("sib_up_a", UP_A, SIB_UP_A, sibling)
    move("sib_down_a", DOWN_A, SIB_DOWN_A, sibling)
    move("far_up_a", UP_A, FAR_A, up, first)
    move("far_down_a", DOWN_A, FAR_A, down, second)
    move("sib_far_a", FAR_A, SIB_FAR_A, sibling)

    def square(i, total):
        tok_copy(i).wait()
        x = tok[i].astype(F32)
        x = x * x
        return total + sum(x[:, j * 128:(j + 1) * 128] for j in range(PART // 128))

    total = lax.fori_loop(0, PARTS, square, jnp.zeros((ROWS, 128), F32))
    factor = lax.rsqrt(jnp.sum(total, axis=1, keepdims=True) * (1.0 / WIDTH) + 1e-5)

    def scale(i, _):
        normed[i] = (tok[i].astype(F32) * factor * gain[i]).astype(BF16)
        return 0

    lax.fori_loop(0, PARTS, scale, 0)

    def project(i, _):
        for c in w_copies(i):
            c.wait()
        x = normed[i]
        pieces = [
            jnp.dot(x, wq_v[i], preferred_element_type=F32),
            jnp.dot(x, wk_v[i], preferred_element_type=F32),
            jnp.dot(x, wv_v[i], preferred_element_type=F32),
        ]
        spans = [(0, 1024), (1024, 1152), (1152, 1280)]

        @pl.when(i == 0)
        def _():
            for (a, b), piece in zip(spans, pieces):
                proj[:, a:b] = piece

        @pl.when(i > 0)
        def _():
            for (a, b), piece in zip(spans, pieces):
                proj[:, a:b] += piece

        @pl.when(i == 4)
        def _():
            for d in range(1, TP):
                a_arrival(d).wait_recv()
            own.wait()
            for name in ("own_across", "own_up", "own_down", "sib_own"):
                moves[name].start()

        return 0

    lax.fori_loop(0, PARTS, project, 0)

    def rotate(u):
        return u * cos_ref[...] + pltpu.roll(u, HEAD // 2, 1) * sin_ref[...]

    for h in range(GROUP):
        u = rotate(proj[:, h * HEAD:(h + 1) * HEAD])
        q[h * ROWS:(h + 1) * ROWS, :] = (u * SCALE).astype(BF16)
    fresh[0] = rotate(proj[:, 1024:1152]).astype(BF16)
    fresh[1] = proj[:, 1152:1280].astype(BF16)

    def attend(h, keys, values, near=None):
        rows = pl.ds(h * ROWS, ROWS)
        scores = lax.dot_general(
            q[rows, :], keys, (((1,), (1,)), ((), ())), preferred_element_type=F32
        )
        if near is not None:
            scores = jnp.where(near, scores, -1e30)
        peak = jnp.max(scores, axis=1, keepdims=True)
        if near is None:
            before = top[rows, :]
            peak = jnp.maximum(before, peak)
            fade = jnp.exp2(before - peak)
            top[rows, :] = peak
            level = peak[:, 0:1]
        else:
            top[rows, :] = jnp.broadcast_to(peak, (ROWS, 128))
            level = peak
        weights = jnp.exp2(scores - level).astype(BF16)
        wide = jnp.concatenate([values, jnp.ones_like(values)], axis=1)
        part = jnp.dot(weights, wide, preferred_element_type=F32)
        if near is None:
            acc[rows, :] = acc[rows, :] * jnp.concatenate([fade, fade], axis=1) + part
        else:
            acc[rows, :] = part

    causal = (
        lax.broadcasted_iota(jnp.int32, (ROWS, ROWS), 1)
        <= lax.broadcasted_iota(jnp.int32, (ROWS, ROWS), 0)
    )
    for h in range(GROUP):
        attend(h, fresh[0], fresh[1], causal)

    def step(i, _):
        @pl.when(i == 0)
        def _():
            moves["sib_own"].wait_recv()

        @pl.when(i == 1)
        def _():
            moves["own_up"].wait_recv()
            moves["own_down"].wait_recv()
            for name in ("far_up", "far_down", "sib_up", "sib_down"):
                moves[name].start()

        @pl.when(i == 2)
        def _():
            moves["own_across"].wait_recv()
            for name in ("across_up", "across_down", "sib_across"):
                moves[name].start()
            moves["sib_up"].wait_recv()
            moves["sib_down"].wait_recv()

        @pl.when(i == 3)
        def _():
            moves["sib_across"].wait_recv()
            moves["far_up"].wait_recv()
            moves["far_down"].wait_recv()
            moves["sib_far"].start()

        @pl.when(i == 4)
        def _():
            moves["sib_far"].wait_recv()

        @pl.when(i == 5)
        def _():
            moves["across_up"].wait_recv()
            moves["across_down"].wait_recv()
            for name in ("far_up_a", "far_down_a", "sib_up_a", "sib_down_a"):
                moves[name].start()

        @pl.when(i == 6)
        def _():
            moves["sib_up_a"].wait_recv()
            moves["sib_down_a"].wait_recv()
            moves["far_up_a"].wait_recv()
            moves["far_down_a"].wait_recv()
            moves["sib_far_a"].start()

        @pl.when(i == 7)
        def _():
            moves["sib_far_a"].wait_recv()

        for j in range(2):
            for h in range(GROUP):
                attend(h, kv[2 * i + j, 0], kv[2 * i + j, 1])
        return 0

    lax.fori_loop(0, ROLLOUT // 2, step, 0)

    live = lax.broadcasted_iota(jnp.int32, (ROWS, HEAD), 0) < length[0]
    for h in range(GROUP):
        rows = pl.ds(h * ROWS, ROWS)
        result = acc[rows, 0:HEAD] / acc[rows, HEAD:2 * HEAD]
        out[:, h * HEAD:(h + 1) * HEAD] = jnp.where(live, result, 0.0).astype(BF16)

    for d in range(1, TP):
        a_copy(d).wait_send()
    for copy in moves.values():
        copy.wait_send()


def shards(tokens, norm_gain, query_weight, key_matrix, value_matrix, prompt_cache, lengths):
    by_head = jnp.transpose(prompt_cache, (2, 0, 1, 3))
    gain = norm_gain.reshape(PARTS, 1, PART)
    cosine, sine = tables()
    hbm = pl.BlockSpec(memory_space=pl.ANY)
    vmem = pl.BlockSpec(memory_space=pltpu.VMEM)
    smem = pl.BlockSpec(memory_space=pltpu.SMEM)
    return pl.pallas_call(
        kernel,
        out_shape=jax.ShapeDtypeStruct((ROWS, GROUP * HEAD), BF16),
        in_specs=[hbm, vmem, hbm, hbm, hbm, hbm, smem, vmem, vmem],
        out_specs=vmem,
        scratch_shapes=[
            pltpu.VMEM((PARTS, ROWS, PART), BF16),
            pltpu.VMEM((PARTS, ROWS, PART), BF16),
            pltpu.VMEM((PARTS, PART, GROUP * HEAD), BF16),
            pltpu.VMEM((PARTS, PART, HEAD), BF16),
            pltpu.VMEM((PARTS, PART, HEAD), BF16),
            pltpu.VMEM((ROWS, (GROUP + 2) * HEAD), F32),
            pltpu.VMEM((ROLLOUT, 2, CHUNK, HEAD), BF16),
            pltpu.VMEM((GROUP * ROWS, HEAD), BF16),
            pltpu.VMEM((2, ROWS, HEAD), BF16),
            pltpu.VMEM((GROUP * ROWS, 128), F32),
            pltpu.VMEM((GROUP * ROWS, 2 * HEAD), F32),
            pltpu.SemaphoreType.DMA((PARTS,)),
            pltpu.SemaphoreType.DMA((3, PARTS)),
            pltpu.SemaphoreType.DMA,
            pltpu.SemaphoreType.DMA((TP - 1,)),
            pltpu.SemaphoreType.DMA((TP - 1,)),
            pltpu.SemaphoreType.DMA((17,)),
            pltpu.SemaphoreType.DMA((17,)),
        ],
        compiler_params=pltpu.CompilerParams(
            collective_id=0, has_side_effects=True, vmem_limit_bytes=62 << 20
        ),
        cost_estimate=pl.CostEstimate(
            flops=23_000_000_000, bytes_accessed=30_000_000, transcendentals=34_000_000
        ),
    )(
        tokens, gain, query_weight, key_matrix, value_matrix, by_head, lengths,
        jnp.asarray(cosine), jnp.asarray(sine),
    )


def solution(mesh):
    placed = (
        P("rollout", None),
        P(),
        P(None, "tp"),
        P(None, "tp"),
        P(None, "tp"),
        P(None, ("rollout", "tp"), None, None),
        P("rollout"),
    )
    return jax.shard_map(
        shards, mesh=mesh, in_specs=placed, out_specs=P("rollout", "tp"), check_vma=False
    )
```

```python
import functools

import jax
import jax.numpy as jnp
import numpy as np
from jax import lax
from jax.experimental import pallas as pl
from jax.experimental.pallas import tpu as pltpu
from jax.sharding import PartitionSpec as P

F32, BF16 = jnp.float32, jnp.bfloat16
MESH = pl.DeviceIdType.MESH
HEAD = 128
ROWS = 256
GROUP = 8
WIDTH = 8192
PARTS = 8
PART = WIDTH // PARTS
TP, ROLLOUT = 8, 16
PIECE = 128
CHUNK = PIECE * TP
PROMPT = CHUNK * ROLLOUT
ROPE_BASE = 500000.0
SCALE = float(HEAD ** -0.5 * np.log2(np.e))

HALF = CHUNK // 2
EARLY = 4
TILE = 2048
SPAN = 256
OFFSETS = ((0, 0), (0, 1), (1, 0), (3, 0), (1, 1), (3, 1), (2, 0), (2, 1))
OWN, NEAR_A, ACROSS, NEAR_B, ACROSS_A, FAR, ACROSS_B, FAR_ACROSS = range(8)
SLOT = {NEAR_A: 1, ACROSS: 3, NEAR_B: 4, ACROSS_A: 7, FAR: 9, ACROSS_B: 10, FAR_ACROSS: 13}
SIBLING_SLOT = (0, 2, 5, 6, 8, 11, 12, 14)


def tables():
    half = HEAD // 2
    frequency = np.power(
        np.float32(ROPE_BASE), -2.0 * np.arange(half, dtype=np.float32) / np.float32(HEAD)
    ).astype(np.float32)
    position = (PROMPT + np.arange(ROWS)).astype(np.float32)
    angles = (position[:, None] * frequency[None, :]).astype(np.float32).astype(np.float64)
    cosine, sine = np.cos(angles), np.sin(angles)
    return (
        np.concatenate([cosine, cosine], axis=1).astype(np.float32),
        np.concatenate([-sine, sine], axis=1).astype(np.float32),
    )


def kernel(
    tokens, gain, wq, wk, wv, cache, length, cos_ref, sin_ref, out,
    tok, normed, wq_v, wk_v, wv_v, proj, raw, wide, by_head, home, kv, q, top, acc,
    tok_sem, w_sem, raw_sem, a_send, a_recv, send, recv,
):
    r, t = lax.axis_index("rollout"), lax.axis_index("tp")
    y, low = r // 4, r % 4
    core, across = r % 2, (r // 2) % 2
    sibling = r + 1 - 2 * core
    partner = r + 2 - 4 * across
    up = ((y + 1) % 4) * 4 + low
    down = ((y + 3) % 4) * 4 + low

    def tp_device(d):
        dz, dx = OFFSETS[d]
        z, x = t // 2, t % 2
        return ((z + dz) % 4) * 2 + (x + dx) % 2

    barrier = pltpu.get_barrier_semaphore()
    for d in range(1, TP):
        pl.semaphore_signal(barrier, inc=1, device_id=(r, tp_device(d)), device_id_type=MESH)
    for other in (sibling, partner, up, down):
        pl.semaphore_signal(barrier, inc=1, device_id=(other, t), device_id_type=MESH)

    raw_copy = pltpu.make_async_copy(cache, raw, raw_sem)
    raw_copy.start()

    def tok_copy(i):
        return pltpu.make_async_copy(
            tokens.at[:, pl.ds(pl.multiple_of(i * PART, PART), PART)], tok.at[i], tok_sem.at[i]
        )

    def w_copies(i):
        rows = pl.ds(pl.multiple_of(i * PART, PART), PART)
        return [
            pltpu.make_async_copy(wq.at[rows], wq_v.at[i], w_sem.at[0, i]),
            pltpu.make_async_copy(wk.at[rows], wk_v.at[i], w_sem.at[1, i]),
            pltpu.make_async_copy(wv.at[rows], wv_v.at[i], w_sem.at[2, i]),
        ]

    def start_loads(i, _):
        tok_copy(i).start()
        return 0

    def start_weights(i, _):
        for c in w_copies(i):
            c.start()
        return 0

    lax.fori_loop(0, PARTS, start_loads, 0)
    lax.fori_loop(0, EARLY, start_weights, 0)

    raw_copy.wait()
    wide[...] = raw[...].astype(F32)
    for g in range(TP):
        piece = wide[pl.ds(g, 2 * PIECE, stride=TP), :].astype(BF16)
        by_head[g, 0] = piece[:PIECE]
        by_head[g, 1] = piece[PIECE:]


    def a_copy(d):
        head = tp_device(d)
        return pltpu.make_async_remote_copy(
            src_ref=by_head.at[head],
            dst_ref=home.at[:, pl.ds(d * PIECE, PIECE)],
            send_sem=a_send.at[d - 1], recv_sem=a_recv.at[d - 1],
            device_id=(r, head), device_id_type=MESH,
        )


    first, second = pl.ds(0, HALF), pl.ds(HALF, HALF)
    quarters = [pl.ds(j * HALF // 2, HALF // 2) for j in range(4)]
    moves = {}

    def spot(block, rows):
        if block == 0:
            return home.at[:, rows]
        return kv.at[SLOT[block], :, rows]

    def move(name, source, source_rows, target, target_rows, device):
        index = len(moves)
        moves[name] = pltpu.make_async_remote_copy(
            src_ref=spot(source, source_rows), dst_ref=spot(target, target_rows),
            send_sem=send.at[index], recv_sem=recv.at[index],
            device_id=(device, t), device_id_type=MESH,
        )

    move("own_a_up", 0, first, NEAR_A, first, up)
    move("own_a_down", 0, first, NEAR_A, second, down)
    move("own_a_across", 0, first, ACROSS, first, partner)
    move("own_b_up", 0, second, NEAR_B, first, up)
    move("own_b_down", 0, second, NEAR_B, second, down)
    move("own_b_across", 0, second, ACROSS, second, partner)
    move("far_a", NEAR_A, first, FAR, first, up)
    move("far_b", NEAR_B, second, FAR, second, down)
    move("across_a_up", ACROSS, first, ACROSS_A, first, up)
    move("across_a_down", ACROSS, first, ACROSS_A, second, down)
    move("up_b_across", NEAR_B, first, ACROSS_B, first, partner)
    move("down_b_across", NEAR_B, second, ACROSS_B, second, partner)
    move("far_b_across", FAR, second, FAR_ACROSS, second, partner)
    move("far_across_up", ACROSS_A, quarters[0], FAR_ACROSS, quarters[0], up)
    move("far_across_down", ACROSS_A, quarters[3], FAR_ACROSS, quarters[1], down)
    whole = pl.ds(0, CHUNK)
    for block in range(8):
        index = len(moves)
        moves["sibling", block] = pltpu.make_async_remote_copy(
            src_ref=spot(block, whole), dst_ref=kv.at[SIBLING_SLOT[block]],
            send_sem=send.at[index], recv_sem=recv.at[index],
            device_id=(sibling, t), device_id_type=MESH,
        )

    def start(*names):
        for name in names:
            moves[name].start()

    def arrived(*names):
        for name in names:
            moves[name].wait_recv()

    def square(i, total):
        tok_copy(i).wait()
        x = tok[i].astype(F32)
        x = x * x
        return total + sum(x[:, j * 128:(j + 1) * 128] for j in range(PART // 128))

    total = lax.fori_loop(0, PARTS, square, jnp.zeros((ROWS, 128), F32))
    factor = lax.rsqrt(jnp.sum(total, axis=1, keepdims=True) * (1.0 / WIDTH) + 1e-5)

    def scale(i, _):
        normed[i] = (tok[i].astype(F32) * factor * gain[i]).astype(BF16)
        return 0

    lax.fori_loop(0, PARTS, scale, 0)

    pl.semaphore_wait(barrier, TP - 1 + 4)
    for d in range(1, TP):
        a_copy(d).start()
    lax.fori_loop(EARLY, PARTS, start_weights, 0)
    home[:, 0:PIECE, :] = by_head[t]

    def project(i, _):
        for c in w_copies(i):
            c.wait()
        x = normed[i]
        pieces = [
            jnp.dot(x, wq_v[i], preferred_element_type=F32),
            jnp.dot(x, wk_v[i], preferred_element_type=F32),
            jnp.dot(x, wv_v[i], preferred_element_type=F32),
        ]
        spans = [(0, 1024), (1024, 1152), (1152, 1280)]

        @pl.when(i == 0)
        def _():
            for (a, b), piece in zip(spans, pieces):
                proj[:, a:b] = piece

        @pl.when(i > 0)
        def _():
            for (a, b), piece in zip(spans, pieces):
                proj[:, a:b] += piece

        @pl.when(i == PARTS - 1)
        def _():
            for d in range(1, 4):
                a_copy(d).wait_recv()
            start("own_a_up", "own_a_down", "own_a_across")

        return 0

    lax.fori_loop(0, PARTS, project, 0)

    def rotate(u):
        return u * cos_ref[...] + pltpu.roll(u, HEAD // 2, 1) * sin_ref[...]

    for h in range(GROUP):
        u = rotate(proj[:, h * HEAD:(h + 1) * HEAD])
        q[h * ROWS:(h + 1) * ROWS, :] = (u * SCALE).astype(BF16)
    home[0, CHUNK:, :] = rotate(proj[:, 1024:1152]).astype(BF16)
    home[1, CHUNK:, :] = proj[:, 1152:1280].astype(BF16)

    for d in range(4, TP):
        a_copy(d).wait_recv()
    start("own_b_up", "own_b_down", "own_b_across", ("sibling", OWN))

    def attend(start, count, keys, values, near=None):
        rows = pl.ds(start, count)
        scores = lax.dot_general(
            q[rows, :], keys, (((1,), (1,)), ((), ())), preferred_element_type=F32
        )
        if near is not None:
            scores = jnp.where(near, scores, -1e30)
        peak = jnp.max(scores, axis=1, keepdims=True)
        if near is None:
            before = top[rows, :]
            peak = jnp.maximum(before, peak)
            fade = jnp.exp2(before - peak)
        else:
            peak = jnp.broadcast_to(peak, (count, 128))
        top[rows, :] = peak
        weights = jnp.concatenate(
            [jnp.exp2(scores[:, j:j + 128] - peak) for j in range(0, SPAN, 128)], axis=1
        ).astype(BF16)
        both = jnp.concatenate([values, jnp.ones_like(values)], axis=1)
        part = jnp.dot(weights, both, preferred_element_type=F32)
        if near is None:
            acc[rows, :] = acc[rows, :] * jnp.concatenate([fade, fade], axis=1) + part
        else:
            acc[rows, :] = part

    def absorb(block):
        for j in range(0, CHUNK, SPAN):
            for start in range(0, GROUP * ROWS, TILE):
                attend(start, TILE, block[0, j:j + SPAN, :], block[1, j:j + SPAN, :])

    causal = (
        lax.broadcasted_iota(jnp.int32, (ROWS, ROWS), 1)
        <= lax.broadcasted_iota(jnp.int32, (ROWS, ROWS), 0)
    )
    for h in range(GROUP):
        attend(h * ROWS, ROWS, home[0, CHUNK:, :], home[1, CHUNK:, :], causal)
    absorb(home)

    def step(i, _):
        @pl.when(i == 0)
        def _():
            arrived("own_a_across")
            start("across_a_up", "across_a_down")
            arrived("own_a_up", "own_a_down")
            start(("sibling", NEAR_A))
            arrived(("sibling", OWN))

        @pl.when(i == 1)
        def _():
            arrived("own_b_across")
            start(("sibling", ACROSS))
            arrived(("sibling", NEAR_A))

        @pl.when(i == 2)
        def _():
            arrived("own_b_up", "own_b_down")
            start("up_b_across", "down_b_across", "far_b", "far_a", ("sibling", NEAR_B))
            arrived(("sibling", ACROSS))

        @pl.when(i == 3)
        def _():
            arrived("across_a_up", "across_a_down")
            start("far_across_up", "far_across_down", ("sibling", ACROSS_A))
            arrived(("sibling", NEAR_B))

        @pl.when(i == 4)
        def _():
            arrived("far_b")
            start("far_b_across")
            arrived("far_a")
            start(("sibling", FAR))
            arrived(("sibling", ACROSS_A))

        @pl.when(i == 5)
        def _():
            arrived("up_b_across", "down_b_across")
            start(("sibling", ACROSS_B))
            arrived(("sibling", FAR))

        @pl.when(i == 6)
        def _():
            arrived("far_across_up", "far_across_down", "far_b_across")
            start(("sibling", FAR_ACROSS))
            arrived(("sibling", ACROSS_B))

        absorb(kv.at[2 * i])
        absorb(kv.at[2 * i + 1])
        return 0

    lax.fori_loop(0, 7, step, 0)

    arrived(("sibling", FAR_ACROSS))
    absorb(kv.at[14])
    live = lax.broadcasted_iota(jnp.int32, (ROWS, HEAD), 0) < length[0]
    for h in range(GROUP):
        rows = pl.ds(h * ROWS, ROWS)
        result = acc[rows, 0:HEAD] / acc[rows, HEAD:2 * HEAD]
        out[:, h * HEAD:(h + 1) * HEAD] = jnp.where(live, result, 0.0).astype(BF16)

    for d in range(1, TP):
        a_copy(d).wait_send()
    for copy in moves.values():
        copy.wait_send()


def shards(tokens, norm_gain, query_weight, key_matrix, value_matrix, prompt_cache, lengths):
    cache = prompt_cache.reshape(2 * PIECE * TP, HEAD)
    gain = norm_gain.reshape(PARTS, 1, PART)
    cosine, sine = tables()
    hbm = pl.BlockSpec(memory_space=pl.ANY)
    vmem = pl.BlockSpec(memory_space=pltpu.VMEM)
    smem = pl.BlockSpec(memory_space=pltpu.SMEM)
    return pl.pallas_call(
        kernel,
        out_shape=jax.ShapeDtypeStruct((ROWS, GROUP * HEAD), BF16),
        in_specs=[hbm, vmem, hbm, hbm, hbm, hbm, smem, vmem, vmem],
        out_specs=vmem,
        scratch_shapes=[
            pltpu.VMEM((PARTS, ROWS, PART), BF16),
            pltpu.VMEM((PARTS, ROWS, PART), BF16),
            pltpu.VMEM((PARTS, PART, GROUP * HEAD), BF16),
            pltpu.VMEM((PARTS, PART, HEAD), BF16),
            pltpu.VMEM((PARTS, PART, HEAD), BF16),
            pltpu.VMEM((ROWS, (GROUP + 2) * HEAD), F32),
            pltpu.VMEM((2 * PIECE * TP, HEAD), BF16),
            pltpu.VMEM((2 * PIECE * TP, HEAD), F32),
            pltpu.VMEM((TP, 2, PIECE, HEAD), BF16),
            pltpu.VMEM((2, CHUNK + ROWS, HEAD), BF16),
            pltpu.VMEM((ROLLOUT - 1, 2, CHUNK, HEAD), BF16),
            pltpu.VMEM((GROUP * ROWS, HEAD), BF16),
            pltpu.VMEM((GROUP * ROWS, 128), F32),
            pltpu.VMEM((GROUP * ROWS, 2 * HEAD), F32),
            pltpu.SemaphoreType.DMA((PARTS,)),
            pltpu.SemaphoreType.DMA((3, PARTS)),
            pltpu.SemaphoreType.DMA,
            pltpu.SemaphoreType.DMA((TP - 1,)),
            pltpu.SemaphoreType.DMA((TP - 1,)),
            pltpu.SemaphoreType.DMA((23,)),
            pltpu.SemaphoreType.DMA((23,)),
        ],
        compiler_params=pltpu.CompilerParams(
            collective_id=0, has_side_effects=True, vmem_limit_bytes=62 << 20
        ),
        cost_estimate=pl.CostEstimate(
            flops=23_000_000_000, bytes_accessed=30_000_000, transcendentals=34_000_000
        ),
    )(
        tokens, gain, query_weight, key_matrix, value_matrix, cache, lengths,
        jnp.asarray(cosine), jnp.asarray(sine),
    )


def solution(mesh):
    placed = (
        P("rollout", None),
        P(),
        P(None, "tp"),
        P(None, "tp"),
        P(None, "tp"),
        P(None, ("rollout", "tp"), None, None),
        P("rollout"),
    )
    return jax.shard_map(
        shards, mesh=mesh, in_specs=placed, out_specs=P("rollout", "tp"), check_vma=False
    )
```

```python
import functools

import jax
import jax.numpy as jnp
import numpy as np
from jax import lax
from jax.experimental import pallas as pl
from jax.experimental.pallas import tpu as pltpu
from jax.sharding import PartitionSpec as P

F32, BF16 = jnp.float32, jnp.bfloat16
MESH = pl.DeviceIdType.MESH
HEAD = 128
ROWS = 256
GROUP = 8
WIDTH = 8192
PARTS = 8
PART = WIDTH // PARTS
TP, ROLLOUT = 8, 16
PIECE = 128
CHUNK = PIECE * TP
PROMPT = CHUNK * ROLLOUT
ROPE_BASE = 500000.0
SCALE = float(HEAD ** -0.5 * np.log2(np.e))

HALF = CHUNK // 2
EARLY = 4
TILE = 2048
SPAN = 256
OFFSETS = ((0, 0), (0, 1), (1, 0), (3, 0), (1, 1), (3, 1), (2, 0), (2, 1))
OWN, NEAR_A, ACROSS, NEAR_B, ACROSS_A, FAR, ACROSS_B, FAR_ACROSS = range(8)
SLOT = {NEAR_A: 1, ACROSS: 3, NEAR_B: 4, ACROSS_A: 7, FAR: 9, ACROSS_B: 10, FAR_ACROSS: 13}
SIBLING_SLOT = (0, 2, 5, 6, 8, 11, 12, 14)


def tables():
    half = HEAD // 2
    frequency = np.power(
        np.float32(ROPE_BASE), -2.0 * np.arange(half, dtype=np.float32) / np.float32(HEAD)
    ).astype(np.float32)
    position = (PROMPT + np.arange(ROWS)).astype(np.float32)
    angles = (position[:, None] * frequency[None, :]).astype(np.float32).astype(np.float64)
    cosine, sine = np.cos(angles), np.sin(angles)
    return (
        np.concatenate([cosine, cosine], axis=1).astype(np.float32),
        np.concatenate([-sine, sine], axis=1).astype(np.float32),
    )


def kernel(
    tokens, gain, wq, wk, wv, cache, cos_ref, sin_ref, out,
    tok, normed, wq_v, wk_v, wv_v, proj, raw, wide, by_head, home, kv, q, top, acc,
    tok_sem, w_sem, raw_sem, a_send, a_recv, send, recv,
):
    r, t = lax.axis_index("rollout"), lax.axis_index("tp")
    y, low = r // 4, r % 4
    core, across = r % 2, (r // 2) % 2
    sibling = r + 1 - 2 * core
    partner = r + 2 - 4 * across
    up = ((y + 1) % 4) * 4 + low
    down = ((y + 3) % 4) * 4 + low

    def tp_device(d):
        dz, dx = OFFSETS[d]
        z, x = t // 2, t % 2
        return ((z + dz) % 4) * 2 + (x + dx) % 2

    barrier = pltpu.get_barrier_semaphore()
    for d in range(1, TP):
        pl.semaphore_signal(barrier, inc=1, device_id=(r, tp_device(d)), device_id_type=MESH)
    for other in (sibling, partner, up, down):
        pl.semaphore_signal(barrier, inc=1, device_id=(other, t), device_id_type=MESH)

    raw_copy = pltpu.make_async_copy(cache, raw, raw_sem)
    raw_copy.start()

    def tok_copy(i):
        return pltpu.make_async_copy(
            tokens.at[:, pl.ds(pl.multiple_of(i * PART, PART), PART)], tok.at[i], tok_sem.at[i]
        )

    def w_copies(i):
        rows = pl.ds(pl.multiple_of(i * PART, PART), PART)
        return [
            pltpu.make_async_copy(wq.at[rows], wq_v.at[i], w_sem.at[0, i]),
            pltpu.make_async_copy(wk.at[rows], wk_v.at[i], w_sem.at[1, i]),
            pltpu.make_async_copy(wv.at[rows], wv_v.at[i], w_sem.at[2, i]),
        ]

    def start_loads(i, _):
        tok_copy(i).start()
        return 0

    def start_weights(i, _):
        for c in w_copies(i):
            c.start()
        return 0

    lax.fori_loop(0, PARTS, start_loads, 0)
    lax.fori_loop(0, EARLY, start_weights, 0)

    raw_copy.wait()
    wide[...] = raw[...].astype(F32)
    for g in range(TP):
        piece = wide[pl.ds(g, 2 * PIECE, stride=TP), :].astype(BF16)
        by_head[g, 0] = piece[:PIECE]
        by_head[g, 1] = piece[PIECE:]


    def a_copy(d):
        head = tp_device(d)
        return pltpu.make_async_remote_copy(
            src_ref=by_head.at[head],
            dst_ref=home.at[:, pl.ds(d * PIECE, PIECE)],
            send_sem=a_send.at[d - 1], recv_sem=a_recv.at[d - 1],
            device_id=(r, head), device_id_type=MESH,
        )


    first, second = pl.ds(0, HALF), pl.ds(HALF, HALF)
    quarters = [pl.ds(j * HALF // 2, HALF // 2) for j in range(4)]
    moves = {}

    def spot(block, rows):
        if block == 0:
            return home.at[:, rows]
        return kv.at[SLOT[block], :, rows]

    def move(name, source, source_rows, target, target_rows, device):
        index = len(moves)
        moves[name] = pltpu.make_async_remote_copy(
            src_ref=spot(source, source_rows), dst_ref=spot(target, target_rows),
            send_sem=send.at[index], recv_sem=recv.at[index],
            device_id=(device, t), device_id_type=MESH,
        )

    move("own_a_up", 0, first, NEAR_A, first, up)
    move("own_a_down", 0, first, NEAR_A, second, down)
    move("own_a_across", 0, first, ACROSS, first, partner)
    move("own_b_up", 0, second, NEAR_B, first, up)
    move("own_b_down", 0, second, NEAR_B, second, down)
    move("own_b_across", 0, second, ACROSS, second, partner)
    move("far_a", NEAR_A, first, FAR, first, up)
    move("far_b", NEAR_B, second, FAR, second, down)
    move("across_a_up", ACROSS, first, ACROSS_A, first, up)
    move("across_a_down", ACROSS, first, ACROSS_A, second, down)
    move("up_b_across", NEAR_B, first, ACROSS_B, first, partner)
    move("down_b_across", NEAR_B, second, ACROSS_B, second, partner)
    move("far_b_across", FAR, second, FAR_ACROSS, second, partner)
    move("far_across_up", ACROSS_A, quarters[0], FAR_ACROSS, quarters[0], up)
    move("far_across_down", ACROSS_A, quarters[3], FAR_ACROSS, quarters[1], down)
    whole = pl.ds(0, CHUNK)
    for block in range(8):
        index = len(moves)
        moves["sibling", block] = pltpu.make_async_remote_copy(
            src_ref=spot(block, whole), dst_ref=kv.at[SIBLING_SLOT[block]],
            send_sem=send.at[index], recv_sem=recv.at[index],
            device_id=(sibling, t), device_id_type=MESH,
        )

    def start(*names):
        for name in names:
            moves[name].start()

    def arrived(*names):
        for name in names:
            moves[name].wait_recv()

    def square(i, total):
        tok_copy(i).wait()
        x = tok[i].astype(F32)
        x = x * x
        return total + sum(x[:, j * 128:(j + 1) * 128] for j in range(PART // 128))

    total = lax.fori_loop(0, PARTS, square, jnp.zeros((ROWS, 128), F32))
    factor = lax.rsqrt(jnp.sum(total, axis=1, keepdims=True) * (1.0 / WIDTH) + 1e-5)

    def scale(i, _):
        normed[i] = (tok[i].astype(F32) * factor * gain[i]).astype(BF16)
        return 0

    lax.fori_loop(0, PARTS, scale, 0)

    pl.semaphore_wait(barrier, TP - 1 + 4)
    for d in range(1, TP):
        a_copy(d).start()
    lax.fori_loop(EARLY, PARTS, start_weights, 0)
    home[:, 0:PIECE, :] = by_head[t]

    def project(i, _):
        for c in w_copies(i):
            c.wait()
        x = normed[i]
        pieces = [
            jnp.dot(x, wq_v[i], preferred_element_type=F32),
            jnp.dot(x, wk_v[i], preferred_element_type=F32),
            jnp.dot(x, wv_v[i], preferred_element_type=F32),
        ]
        spans = [(0, 1024), (1024, 1152), (1152, 1280)]

        @pl.when(i == 0)
        def _():
            for (a, b), piece in zip(spans, pieces):
                proj[:, a:b] = piece

        @pl.when(i > 0)
        def _():
            for (a, b), piece in zip(spans, pieces):
                proj[:, a:b] += piece

        @pl.when(i == PARTS - 2)
        def _():
            for d in range(1, 4):
                a_copy(d).wait_recv()
            start("own_a_up", "own_a_down", "own_a_across")

        return 0

    lax.fori_loop(0, PARTS, project, 0)

    def rotate(u):
        return u * cos_ref[...] + pltpu.roll(u, HEAD // 2, 1) * sin_ref[...]

    for h in range(GROUP):
        u = rotate(proj[:, h * HEAD:(h + 1) * HEAD])
        q[h * ROWS:(h + 1) * ROWS, :] = (u * SCALE).astype(BF16)
    home[0, CHUNK:, :] = rotate(proj[:, 1024:1152]).astype(BF16)
    home[1, CHUNK:, :] = proj[:, 1152:1280].astype(BF16)

    for d in range(4, TP):
        a_copy(d).wait_recv()
    start("own_b_up", "own_b_down", "own_b_across", ("sibling", OWN))

    def attend(start, count, keys, values, near=None):
        rows = pl.ds(start, count)
        scores = lax.dot_general(
            q[rows, :], keys, (((1,), (1,)), ((), ())), preferred_element_type=F32
        )
        if near is not None:
            scores = jnp.where(near, scores, -1e30)
        peak = jnp.max(scores, axis=1, keepdims=True)
        if near is None:
            before = top[rows, :]
            peak = jnp.maximum(before, peak)
            fade = jnp.exp2(before - peak)
        else:
            peak = jnp.broadcast_to(peak, (count, 128))
        top[rows, :] = peak
        weights = jnp.concatenate(
            [jnp.exp2(scores[:, j:j + 128] - peak) for j in range(0, SPAN, 128)], axis=1
        ).astype(BF16)
        both = jnp.concatenate([values, jnp.ones_like(values)], axis=1)
        part = jnp.dot(weights, both, preferred_element_type=F32)
        if near is None:
            acc[rows, :] = acc[rows, :] * jnp.concatenate([fade, fade], axis=1) + part
        else:
            acc[rows, :] = part

    def absorb(block):
        for j in range(0, CHUNK, SPAN):
            for start in range(0, GROUP * ROWS, TILE):
                attend(start, TILE, block[0, j:j + SPAN, :], block[1, j:j + SPAN, :])

    causal = (
        lax.broadcasted_iota(jnp.int32, (ROWS, ROWS), 1)
        <= lax.broadcasted_iota(jnp.int32, (ROWS, ROWS), 0)
    )
    for h in range(GROUP):
        attend(h * ROWS, ROWS, home[0, CHUNK:, :], home[1, CHUNK:, :], causal)
    absorb(home)

    def step(i, _):
        @pl.when(i == 0)
        def _():
            arrived("own_a_across")
            start("across_a_up", "across_a_down")
            arrived("own_a_up", "own_a_down")
            start(("sibling", NEAR_A))
            arrived(("sibling", OWN))

        @pl.when(i == 1)
        def _():
            arrived("own_b_across")
            start(("sibling", ACROSS))
            arrived(("sibling", NEAR_A))

        @pl.when(i == 2)
        def _():
            arrived("own_b_up", "own_b_down")
            start("up_b_across", "down_b_across", "far_b", "far_a", ("sibling", NEAR_B))
            arrived(("sibling", ACROSS))

        @pl.when(i == 3)
        def _():
            arrived("across_a_up", "across_a_down")
            start("far_across_up", "far_across_down", ("sibling", ACROSS_A))
            arrived(("sibling", NEAR_B))

        @pl.when(i == 4)
        def _():
            arrived("far_b")
            start("far_b_across")
            arrived("far_a")
            start(("sibling", FAR))
            arrived(("sibling", ACROSS_A))

        @pl.when(i == 5)
        def _():
            arrived("up_b_across", "down_b_across")
            start(("sibling", ACROSS_B))
            arrived(("sibling", FAR))

        @pl.when(i == 6)
        def _():
            arrived("far_across_up", "far_across_down", "far_b_across")
            start(("sibling", FAR_ACROSS))
            arrived(("sibling", ACROSS_B))

        absorb(kv.at[2 * i])
        absorb(kv.at[2 * i + 1])
        return 0

    lax.fori_loop(0, 7, step, 0)

    arrived(("sibling", FAR_ACROSS))
    absorb(kv.at[14])
    for h in range(GROUP):
        rows = pl.ds(h * ROWS, ROWS)
        result = acc[rows, 0:HEAD] / acc[rows, HEAD:2 * HEAD]
        out[:, h * HEAD:(h + 1) * HEAD] = result.astype(BF16)

    for d in range(1, TP):
        a_copy(d).wait_send()
    for copy in moves.values():
        copy.wait_send()


def shards(tokens, norm_gain, query_weight, key_matrix, value_matrix, prompt_cache, lengths):
    cache = prompt_cache.reshape(2 * PIECE * TP, HEAD)
    gain = norm_gain.reshape(PARTS, 1, PART)
    cosine, sine = tables()
    hbm = pl.BlockSpec(memory_space=pl.ANY)
    vmem = pl.BlockSpec(memory_space=pltpu.VMEM)
    context = pl.pallas_call(
        kernel,
        out_shape=jax.ShapeDtypeStruct((ROWS, GROUP * HEAD), BF16),
        in_specs=[hbm, vmem, hbm, hbm, hbm, hbm, vmem, vmem],
        out_specs=vmem,
        scratch_shapes=[
            pltpu.VMEM((PARTS, ROWS, PART), BF16),
            pltpu.VMEM((PARTS, ROWS, PART), BF16),
            pltpu.VMEM((PARTS, PART, GROUP * HEAD), BF16),
            pltpu.VMEM((PARTS, PART, HEAD), BF16),
            pltpu.VMEM((PARTS, PART, HEAD), BF16),
            pltpu.VMEM((ROWS, (GROUP + 2) * HEAD), F32),
            pltpu.VMEM((2 * PIECE * TP, HEAD), BF16),
            pltpu.VMEM((2 * PIECE * TP, HEAD), F32),
            pltpu.VMEM((TP, 2, PIECE, HEAD), BF16),
            pltpu.VMEM((2, CHUNK + ROWS, HEAD), BF16),
            pltpu.VMEM((ROLLOUT - 1, 2, CHUNK, HEAD), BF16),
            pltpu.VMEM((GROUP * ROWS, HEAD), BF16),
            pltpu.VMEM((GROUP * ROWS, 128), F32),
            pltpu.VMEM((GROUP * ROWS, 2 * HEAD), F32),
            pltpu.SemaphoreType.DMA((PARTS,)),
            pltpu.SemaphoreType.DMA((3, PARTS)),
            pltpu.SemaphoreType.DMA,
            pltpu.SemaphoreType.DMA((TP - 1,)),
            pltpu.SemaphoreType.DMA((TP - 1,)),
            pltpu.SemaphoreType.DMA((23,)),
            pltpu.SemaphoreType.DMA((23,)),
        ],
        compiler_params=pltpu.CompilerParams(
            collective_id=0, has_side_effects=True, vmem_limit_bytes=62 << 20
        ),
        cost_estimate=pl.CostEstimate(
            flops=23_000_000_000, bytes_accessed=30_000_000, transcendentals=34_000_000
        ),
    )(
        tokens, gain, query_weight, key_matrix, value_matrix, cache,
        jnp.asarray(cosine), jnp.asarray(sine),
    )
    live = jnp.arange(ROWS)[:, None] < lengths[0]
    return jnp.where(live, context, jnp.zeros_like(context))


def solution(mesh):
    placed = (
        P("rollout", None),
        P(),
        P(None, "tp"),
        P(None, "tp"),
        P(None, "tp"),
        P(None, ("rollout", "tp"), None, None),
        P("rollout"),
    )
    return jax.shard_map(
        shards, mesh=mesh, in_specs=placed, out_specs=P("rollout", "tp"), check_vma=False
    )
```

```python
import functools

import jax
import jax.numpy as jnp
import numpy as np
from jax import lax
from jax.experimental import pallas as pl
from jax.experimental.pallas import tpu as pltpu
from jax.sharding import PartitionSpec as P

F32, BF16 = jnp.float32, jnp.bfloat16
MESH = pl.DeviceIdType.MESH
HEAD = 128
ROWS = 256
GROUP = 8
WIDTH = 8192
PARTS = 8
PART = WIDTH // PARTS
TP, ROLLOUT = 8, 16
PIECE = 128
CHUNK = PIECE * TP
PROMPT = CHUNK * ROLLOUT
ROPE_BASE = 500000.0
SCALE = float(HEAD ** -0.5 * np.log2(np.e))

HALF = CHUNK // 2
EARLY = 6
TILE = 2048
SPAN = 256
OFFSETS = ((0, 0), (0, 1), (1, 0), (3, 0), (1, 1), (3, 1), (2, 0), (2, 1))
OWN, NEAR_A, ACROSS, NEAR_B, ACROSS_A, FAR, ACROSS_B, FAR_ACROSS = range(8)
SLOT = {NEAR_A: 1, ACROSS: 3, NEAR_B: 4, ACROSS_A: 7, FAR: 9, ACROSS_B: 10, FAR_ACROSS: 13}
SIBLING_SLOT = (0, 2, 5, 6, 8, 11, 12, 14)


def tables():
    half = HEAD // 2
    frequency = np.power(
        np.float32(ROPE_BASE), -2.0 * np.arange(half, dtype=np.float32) / np.float32(HEAD)
    ).astype(np.float32)
    position = (PROMPT + np.arange(ROWS)).astype(np.float32)
    angles = (position[:, None] * frequency[None, :]).astype(np.float32).astype(np.float64)
    cosine, sine = np.cos(angles), np.sin(angles)
    return (
        np.concatenate([cosine, cosine], axis=1).astype(np.float32),
        np.concatenate([-sine, sine], axis=1).astype(np.float32),
    )


def kernel(
    tokens, gain_h, wq, wk, wv, cache, cos_h, sin_h, out,
    gain, cos_ref, sin_ref, tok, normed, wq_v, wk_v, wv_v, proj, raw, wide, by_head, home, kv, q, top, acc,
    small_sem, tok_sem, w_sem, raw_sem, a_send, a_recv, send, recv,
):
    r, t = lax.axis_index("rollout"), lax.axis_index("tp")
    y, low = r // 4, r % 4
    core, across = r % 2, (r // 2) % 2
    sibling = r + 1 - 2 * core
    partner = r + 2 - 4 * across
    up = ((y + 1) % 4) * 4 + low
    down = ((y + 3) % 4) * 4 + low

    def tp_device(d):
        dz, dx = OFFSETS[d]
        z, x = t // 2, t % 2
        return ((z + dz) % 4) * 2 + (x + dx) % 2

    barrier = pltpu.get_barrier_semaphore()
    for d in range(1, TP):
        pl.semaphore_signal(barrier, inc=1, device_id=(r, tp_device(d)), device_id_type=MESH)
    for other in (sibling, partner, up, down):
        pl.semaphore_signal(barrier, inc=1, device_id=(other, t), device_id_type=MESH)

    raw_copy = pltpu.make_async_copy(cache, raw, raw_sem)
    raw_copy.start()

    def tok_copy(i):
        return pltpu.make_async_copy(
            tokens.at[:, pl.ds(pl.multiple_of(i * PART, PART), PART)], tok.at[i], tok_sem.at[i]
        )

    def w_copies(i):
        rows = pl.ds(pl.multiple_of(i * PART, PART), PART)
        return [
            pltpu.make_async_copy(wq.at[rows], wq_v.at[i], w_sem.at[0, i]),
            pltpu.make_async_copy(wk.at[rows], wk_v.at[i], w_sem.at[1, i]),
            pltpu.make_async_copy(wv.at[rows], wv_v.at[i], w_sem.at[2, i]),
        ]

    def start_loads(i, _):
        tok_copy(i).start()
        return 0

    def start_weights(i, _):
        for c in w_copies(i):
            c.start()
        return 0

    lax.fori_loop(0, PARTS, start_loads, 0)
    small = [
        pltpu.make_async_copy(gain_h, gain, small_sem.at[0]),
        pltpu.make_async_copy(cos_h, cos_ref, small_sem.at[1]),
        pltpu.make_async_copy(sin_h, sin_ref, small_sem.at[2]),
    ]
    for c in small:
        c.start()
    lax.fori_loop(0, EARLY, start_weights, 0)

    raw_copy.wait()
    wide[...] = raw[...].astype(F32)
    for g in range(TP):
        piece = wide[pl.ds(g, 2 * PIECE, stride=TP), :].astype(BF16)
        by_head[g, 0] = piece[:PIECE]
        by_head[g, 1] = piece[PIECE:]


    def a_copy(d):
        head = tp_device(d)
        return pltpu.make_async_remote_copy(
            src_ref=by_head.at[head],
            dst_ref=home.at[:, pl.ds(d * PIECE, PIECE)],
            send_sem=a_send.at[d - 1], recv_sem=a_recv.at[d - 1],
            device_id=(r, head), device_id_type=MESH,
        )


    first, second = pl.ds(0, HALF), pl.ds(HALF, HALF)
    quarters = [pl.ds(j * HALF // 2, HALF // 2) for j in range(4)]
    moves = {}

    def spot(block, rows):
        if block == 0:
            return home.at[:, rows]
        return kv.at[SLOT[block], :, rows]

    def move(name, source, source_rows, target, target_rows, device):
        index = len(moves)
        moves[name] = pltpu.make_async_remote_copy(
            src_ref=spot(source, source_rows), dst_ref=spot(target, target_rows),
            send_sem=send.at[index], recv_sem=recv.at[index],
            device_id=(device, t), device_id_type=MESH,
        )

    move("own_a_up", 0, first, NEAR_A, first, up)
    move("own_a_down", 0, first, NEAR_A, second, down)
    move("own_a_across", 0, first, ACROSS, first, partner)
    move("own_b_up", 0, second, NEAR_B, first, up)
    move("own_b_down", 0, second, NEAR_B, second, down)
    move("own_b_across", 0, second, ACROSS, second, partner)
    move("far_a", NEAR_A, first, FAR, first, up)
    move("far_b", NEAR_B, second, FAR, second, down)
    move("across_a_up", ACROSS, first, ACROSS_A, first, up)
    move("across_a_down", ACROSS, first, ACROSS_A, second, down)
    move("up_b_across", NEAR_B, first, ACROSS_B, first, partner)
    move("down_b_across", NEAR_B, second, ACROSS_B, second, partner)
    move("far_b_across", FAR, second, FAR_ACROSS, second, partner)
    move("far_across_up", ACROSS_A, quarters[0], FAR_ACROSS, quarters[0], up)
    move("far_across_down", ACROSS_A, quarters[3], FAR_ACROSS, quarters[1], down)
    whole = pl.ds(0, CHUNK)
    for block in range(8):
        index = len(moves)
        moves["sibling", block] = pltpu.make_async_remote_copy(
            src_ref=spot(block, whole), dst_ref=kv.at[SIBLING_SLOT[block]],
            send_sem=send.at[index], recv_sem=recv.at[index],
            device_id=(sibling, t), device_id_type=MESH,
        )

    def start(*names):
        for name in names:
            moves[name].start()

    def arrived(*names):
        for name in names:
            moves[name].wait_recv()

    def square(i, total):
        tok_copy(i).wait()
        x = tok[i].astype(F32)
        x = x * x
        return total + sum(x[:, j * 128:(j + 1) * 128] for j in range(PART // 128))

    total = lax.fori_loop(0, PARTS, square, jnp.zeros((ROWS, 128), F32))
    factor = lax.rsqrt(jnp.sum(total, axis=1, keepdims=True) * (1.0 / WIDTH) + 1e-5)

    def scale(i, _):
        normed[i] = (tok[i].astype(F32) * factor * gain[i]).astype(BF16)
        return 0

    for c in small:
        c.wait()
    lax.fori_loop(0, PARTS, scale, 0)

    pl.semaphore_wait(barrier, TP - 1 + 4)
    for d in range(1, TP):
        a_copy(d).start()
    lax.fori_loop(EARLY, PARTS, start_weights, 0)
    home[:, 0:PIECE, :] = by_head[t]

    def project(i, _):
        for c in w_copies(i):
            c.wait()
        x = normed[i]
        pieces = [
            jnp.dot(x, wq_v[i], preferred_element_type=F32),
            jnp.dot(x, wk_v[i], preferred_element_type=F32),
            jnp.dot(x, wv_v[i], preferred_element_type=F32),
        ]
        spans = [(0, 1024), (1024, 1152), (1152, 1280)]

        @pl.when(i == 0)
        def _():
            for (a, b), piece in zip(spans, pieces):
                proj[:, a:b] = piece

        @pl.when(i > 0)
        def _():
            for (a, b), piece in zip(spans, pieces):
                proj[:, a:b] += piece

        @pl.when(i == PARTS - 2)
        def _():
            for d in range(1, 4):
                a_copy(d).wait_recv()
            start("own_a_up", "own_a_down", "own_a_across")

        return 0

    lax.fori_loop(0, PARTS, project, 0)

    def rotate(u):
        return u * cos_ref[...] + pltpu.roll(u, HEAD // 2, 1) * sin_ref[...]

    for h in range(GROUP):
        u = rotate(proj[:, h * HEAD:(h + 1) * HEAD])
        q[h * ROWS:(h + 1) * ROWS, :] = (u * SCALE).astype(BF16)
    home[0, CHUNK:, :] = rotate(proj[:, 1024:1152]).astype(BF16)
    home[1, CHUNK:, :] = proj[:, 1152:1280].astype(BF16)

    for d in range(4, TP):
        a_copy(d).wait_recv()
    start("own_b_up", "own_b_down", "own_b_across", ("sibling", OWN))

    def attend(start, count, keys, values, near=None):
        rows = pl.ds(start, count)
        scores = lax.dot_general(
            q[rows, :], keys, (((1,), (1,)), ((), ())), preferred_element_type=F32
        )
        if near is not None:
            scores = jnp.where(near, scores, -1e30)
        peak = jnp.max(scores, axis=1, keepdims=True)
        if near is None:
            before = top[rows, :]
            peak = jnp.maximum(before, peak)
            fade = jnp.exp2(before - peak)
        else:
            peak = jnp.broadcast_to(peak, (count, 128))
        top[rows, :] = peak
        weights = jnp.concatenate(
            [jnp.exp2(scores[:, j:j + 128] - peak) for j in range(0, SPAN, 128)], axis=1
        ).astype(BF16)
        both = jnp.concatenate([values, jnp.ones_like(values)], axis=1)
        part = jnp.dot(weights, both, preferred_element_type=F32)
        if near is None:
            acc[rows, :] = acc[rows, :] * jnp.concatenate([fade, fade], axis=1) + part
        else:
            acc[rows, :] = part

    def absorb(block):
        for j in range(0, CHUNK, SPAN):
            for start in range(0, GROUP * ROWS, TILE):
                attend(start, TILE, block[0, j:j + SPAN, :], block[1, j:j + SPAN, :])

    causal = (
        lax.broadcasted_iota(jnp.int32, (ROWS, ROWS), 1)
        <= lax.broadcasted_iota(jnp.int32, (ROWS, ROWS), 0)
    )
    for h in range(GROUP):
        attend(h * ROWS, ROWS, home[0, CHUNK:, :], home[1, CHUNK:, :], causal)
    absorb(home)

    def step(i, _):
        @pl.when(i == 0)
        def _():
            arrived("own_a_across")
            start("across_a_up", "across_a_down")
            arrived("own_a_up", "own_a_down")
            start(("sibling", NEAR_A))
            arrived(("sibling", OWN))

        @pl.when(i == 1)
        def _():
            arrived("own_b_across")
            start(("sibling", ACROSS))
            arrived(("sibling", NEAR_A))

        @pl.when(i == 2)
        def _():
            arrived("own_b_up", "own_b_down")
            start("up_b_across", "down_b_across", "far_b", "far_a", ("sibling", NEAR_B))
            arrived(("sibling", ACROSS))

        @pl.when(i == 3)
        def _():
            arrived("across_a_up", "across_a_down")
            start("far_across_up", "far_across_down", ("sibling", ACROSS_A))
            arrived(("sibling", NEAR_B))

        @pl.when(i == 4)
        def _():
            arrived("far_b")
            start("far_b_across")
            arrived("far_a")
            start(("sibling", FAR))
            arrived(("sibling", ACROSS_A))

        @pl.when(i == 5)
        def _():
            arrived("up_b_across", "down_b_across")
            start(("sibling", ACROSS_B))
            arrived(("sibling", FAR))

        @pl.when(i == 6)
        def _():
            arrived("far_across_up", "far_across_down", "far_b_across")
            start(("sibling", FAR_ACROSS))
            arrived(("sibling", ACROSS_B))

        absorb(kv.at[2 * i])
        absorb(kv.at[2 * i + 1])
        return 0

    lax.fori_loop(0, 7, step, 0)

    arrived(("sibling", FAR_ACROSS))
    absorb(kv.at[14])
    for h in range(GROUP):
        rows = pl.ds(h * ROWS, ROWS)
        result = acc[rows, 0:HEAD] / acc[rows, HEAD:2 * HEAD]
        out[:, h * HEAD:(h + 1) * HEAD] = result.astype(BF16)

    for d in range(1, TP):
        a_copy(d).wait_send()
    for copy in moves.values():
        copy.wait_send()


def shards(tokens, norm_gain, query_weight, key_matrix, value_matrix, prompt_cache, lengths):
    cache = prompt_cache.reshape(2 * PIECE * TP, HEAD)
    gain = norm_gain.reshape(PARTS, 1, PART)
    cosine, sine = tables()
    hbm = pl.BlockSpec(memory_space=pl.ANY)
    vmem = pl.BlockSpec(memory_space=pltpu.VMEM)
    context = pl.pallas_call(
        kernel,
        out_shape=jax.ShapeDtypeStruct((ROWS, GROUP * HEAD), BF16),
        in_specs=[hbm] * 8,
        out_specs=vmem,
        scratch_shapes=[
            pltpu.VMEM((PARTS, 1, PART), F32),
            pltpu.VMEM((ROWS, HEAD), F32),
            pltpu.VMEM((ROWS, HEAD), F32),
            pltpu.VMEM((PARTS, ROWS, PART), BF16),
            pltpu.VMEM((PARTS, ROWS, PART), BF16),
            pltpu.VMEM((PARTS, PART, GROUP * HEAD), BF16),
            pltpu.VMEM((PARTS, PART, HEAD), BF16),
            pltpu.VMEM((PARTS, PART, HEAD), BF16),
            pltpu.VMEM((ROWS, (GROUP + 2) * HEAD), F32),
            pltpu.VMEM((2 * PIECE * TP, HEAD), BF16),
            pltpu.VMEM((2 * PIECE * TP, HEAD), F32),
            pltpu.VMEM((TP, 2, PIECE, HEAD), BF16),
            pltpu.VMEM((2, CHUNK + ROWS, HEAD), BF16),
            pltpu.VMEM((ROLLOUT - 1, 2, CHUNK, HEAD), BF16),
            pltpu.VMEM((GROUP * ROWS, HEAD), BF16),
            pltpu.VMEM((GROUP * ROWS, 128), F32),
            pltpu.VMEM((GROUP * ROWS, 2 * HEAD), F32),
            pltpu.SemaphoreType.DMA((3,)),
            pltpu.SemaphoreType.DMA((PARTS,)),
            pltpu.SemaphoreType.DMA((3, PARTS)),
            pltpu.SemaphoreType.DMA,
            pltpu.SemaphoreType.DMA((TP - 1,)),
            pltpu.SemaphoreType.DMA((TP - 1,)),
            pltpu.SemaphoreType.DMA((23,)),
            pltpu.SemaphoreType.DMA((23,)),
        ],
        compiler_params=pltpu.CompilerParams(
            collective_id=0, has_side_effects=True, vmem_limit_bytes=62 << 20
        ),
        cost_estimate=pl.CostEstimate(
            flops=23_000_000_000, bytes_accessed=30_000_000, transcendentals=34_000_000
        ),
    )(
        tokens, gain, query_weight, key_matrix, value_matrix, cache,
        jnp.asarray(cosine), jnp.asarray(sine),
    )
    live = jnp.arange(ROWS)[:, None] < lengths[0]
    return jnp.where(live, context, jnp.zeros_like(context))


def solution(mesh):
    placed = (
        P("rollout", None),
        P(),
        P(None, "tp"),
        P(None, "tp"),
        P(None, "tp"),
        P(None, ("rollout", "tp"), None, None),
        P("rollout"),
    )
    return jax.shard_map(
        shards, mesh=mesh, in_specs=placed, out_specs=P("rollout", "tp"), check_vma=False
    )
```

```python
import functools

import jax
import jax.numpy as jnp
import numpy as np
from jax import lax
from jax.experimental import pallas as pl
from jax.experimental.pallas import tpu as pltpu
from jax.sharding import PartitionSpec as P

F32, BF16 = jnp.float32, jnp.bfloat16
MESH = pl.DeviceIdType.MESH
HEAD = 128
ROWS = 256
GROUP = 8
WIDTH = 8192
PARTS = 8
PART = WIDTH // PARTS
TP, ROLLOUT = 8, 16
PIECE = 128
CHUNK = PIECE * TP
PROMPT = CHUNK * ROLLOUT
ROPE_BASE = 500000.0
SCALE = float(HEAD ** -0.5 * np.log2(np.e))

HALF = CHUNK // 2
EARLY = 6
TILE = 2048
SPAN = 256
OFFSETS = ((0, 0), (0, 1), (1, 0), (3, 0), (1, 1), (3, 1), (2, 0), (2, 1))
OWN, NEAR_A, ACROSS, NEAR_B, ACROSS_A, FAR, ACROSS_B, FAR_ACROSS = range(8)
SLOT = {NEAR_A: 1, ACROSS: 3, NEAR_B: 4, ACROSS_A: 7, FAR: 9, ACROSS_B: 10, FAR_ACROSS: 13}
SIBLING_SLOT = (0, 2, 5, 6, 8, 11, 12, 14)


def tables():
    half = HEAD // 2
    frequency = np.power(
        np.float32(ROPE_BASE), -2.0 * np.arange(half, dtype=np.float32) / np.float32(HEAD)
    ).astype(np.float32)
    position = (PROMPT + np.arange(ROWS)).astype(np.float32)
    angles = (position[:, None] * frequency[None, :]).astype(np.float32).astype(np.float64)
    cosine, sine = np.cos(angles), np.sin(angles)
    return (
        np.concatenate([cosine, cosine], axis=1).astype(np.float32),
        np.concatenate([-sine, sine], axis=1).astype(np.float32),
    )


def kernel(
    tokens, gain_h, wq, wk, wv, cache, cos_h, sin_h, out,
    gain, cos_ref, sin_ref, tok, normed, wq_v, wk_v, wv_v, proj, raw, wide, by_head, home, kv, q, top, acc,
    small_sem, tok_sem, w_sem, raw_sem, a_send, a_recv, send, recv,
):
    r, t = lax.axis_index("rollout"), lax.axis_index("tp")
    y, low = r // 4, r % 4
    core, across = r % 2, (r // 2) % 2
    sibling = r + 1 - 2 * core
    partner = r + 2 - 4 * across
    up = ((y + 1) % 4) * 4 + low
    down = ((y + 3) % 4) * 4 + low

    def tp_device(d):
        dz, dx = OFFSETS[d]
        z, x = t // 2, t % 2
        return ((z + dz) % 4) * 2 + (x + dx) % 2

    barrier = pltpu.get_barrier_semaphore()
    for d in range(1, TP):
        pl.semaphore_signal(barrier, inc=1, device_id=(r, tp_device(d)), device_id_type=MESH)
    for other in (sibling, partner, up, down):
        pl.semaphore_signal(barrier, inc=1, device_id=(other, t), device_id_type=MESH)

    raw_copy = pltpu.make_async_copy(cache, raw, raw_sem)
    raw_copy.start()

    def tok_copy(i):
        return pltpu.make_async_copy(
            tokens.at[:, pl.ds(pl.multiple_of(i * PART, PART), PART)], tok.at[i], tok_sem.at[i]
        )

    def w_copies(i):
        rows = pl.ds(pl.multiple_of(i * PART, PART), PART)
        return [
            pltpu.make_async_copy(wq.at[rows], wq_v.at[i], w_sem.at[0, i]),
            pltpu.make_async_copy(wk.at[rows], wk_v.at[i], w_sem.at[1, i]),
            pltpu.make_async_copy(wv.at[rows], wv_v.at[i], w_sem.at[2, i]),
        ]

    def start_loads(i, _):
        tok_copy(i).start()
        return 0

    def start_weights(i, _):
        for c in w_copies(i):
            c.start()
        return 0

    lax.fori_loop(0, PARTS, start_loads, 0)
    small = [
        pltpu.make_async_copy(gain_h, gain, small_sem.at[0]),
        pltpu.make_async_copy(cos_h, cos_ref, small_sem.at[1]),
        pltpu.make_async_copy(sin_h, sin_ref, small_sem.at[2]),
    ]
    for c in small:
        c.start()
    lax.fori_loop(0, EARLY, start_weights, 0)

    raw_copy.wait()
    wide[...] = raw[...].astype(F32)
    for g in range(TP):
        piece = wide[pl.ds(g, 2 * PIECE, stride=TP), :].astype(BF16)
        by_head[g, 0] = piece[:PIECE]
        by_head[g, 1] = piece[PIECE:]


    def a_copy(d):
        head = tp_device(d)
        return pltpu.make_async_remote_copy(
            src_ref=by_head.at[head],
            dst_ref=home.at[:, pl.ds(d * PIECE, PIECE)],
            send_sem=a_send.at[d - 1], recv_sem=a_recv.at[d - 1],
            device_id=(r, head), device_id_type=MESH,
        )


    first, second = pl.ds(0, HALF), pl.ds(HALF, HALF)
    quarters = [pl.ds(j * HALF // 2, HALF // 2) for j in range(4)]
    moves = {}

    def spot(block, rows):
        if block == 0:
            return home.at[:, rows]
        return kv.at[SLOT[block], :, rows]

    def move(name, source, source_rows, target, target_rows, device):
        index = len(moves)
        moves[name] = pltpu.make_async_remote_copy(
            src_ref=spot(source, source_rows), dst_ref=spot(target, target_rows),
            send_sem=send.at[index], recv_sem=recv.at[index],
            device_id=(device, t), device_id_type=MESH,
        )

    move("own_a_up", 0, first, NEAR_A, first, up)
    move("own_a_down", 0, first, NEAR_A, second, down)
    move("own_a_across", 0, first, ACROSS, first, partner)
    move("own_b_up", 0, second, NEAR_B, first, up)
    move("own_b_down", 0, second, NEAR_B, second, down)
    move("own_b_across", 0, second, ACROSS, second, partner)
    move("far_a", NEAR_A, first, FAR, first, up)
    move("far_b", NEAR_B, second, FAR, second, down)
    move("across_a_up", ACROSS, first, ACROSS_A, first, up)
    move("across_a_down", ACROSS, first, ACROSS_A, second, down)
    move("up_b_across", NEAR_B, first, ACROSS_B, first, partner)
    move("down_b_across", NEAR_B, second, ACROSS_B, second, partner)
    move("far_b_across", FAR, second, FAR_ACROSS, second, partner)
    move("far_across_up", ACROSS_A, quarters[0], FAR_ACROSS, quarters[0], up)
    move("far_across_down", ACROSS_A, quarters[3], FAR_ACROSS, quarters[1], down)
    whole = pl.ds(0, CHUNK)
    for block in range(8):
        index = len(moves)
        moves["sibling", block] = pltpu.make_async_remote_copy(
            src_ref=spot(block, whole), dst_ref=kv.at[SIBLING_SLOT[block]],
            send_sem=send.at[index], recv_sem=recv.at[index],
            device_id=(sibling, t), device_id_type=MESH,
        )

    def start(*names):
        for name in names:
            moves[name].start()

    def arrived(*names):
        for name in names:
            moves[name].wait_recv()

    def square(i, total):
        tok_copy(i).wait()
        x = tok[i].astype(F32)
        x = x * x
        return total + sum(x[:, j * 128:(j + 1) * 128] for j in range(PART // 128))

    total = lax.fori_loop(0, PARTS, square, jnp.zeros((ROWS, 128), F32))
    factor = lax.rsqrt(jnp.sum(total, axis=1, keepdims=True) * (1.0 / WIDTH) + 1e-5)

    def scale(i, _):
        normed[i] = (tok[i].astype(F32) * factor * gain[i]).astype(BF16)
        return 0

    pl.semaphore_wait(barrier, TP - 1 + 4)
    for d in range(1, TP):
        a_copy(d).start()
    lax.fori_loop(EARLY, PARTS, start_weights, 0)
    home[:, 0:PIECE, :] = by_head[t]

    for c in small:
        c.wait()
    lax.fori_loop(0, PARTS, scale, 0)


    def project(i, _):
        for c in w_copies(i):
            c.wait()
        x = normed[i]
        pieces = [
            jnp.dot(x, wq_v[i], preferred_element_type=F32),
            jnp.dot(x, wk_v[i], preferred_element_type=F32),
            jnp.dot(x, wv_v[i], preferred_element_type=F32),
        ]
        spans = [(0, 1024), (1024, 1152), (1152, 1280)]

        @pl.when(i == 0)
        def _():
            for (a, b), piece in zip(spans, pieces):
                proj[:, a:b] = piece

        @pl.when(i > 0)
        def _():
            for (a, b), piece in zip(spans, pieces):
                proj[:, a:b] += piece

        @pl.when(i == PARTS - 2)
        def _():
            for d in range(1, 4):
                a_copy(d).wait_recv()
            start("own_a_up", "own_a_down", "own_a_across")

        return 0

    lax.fori_loop(0, PARTS, project, 0)

    def rotate(u):
        return u * cos_ref[...] + pltpu.roll(u, HEAD // 2, 1) * sin_ref[...]

    for h in range(GROUP):
        u = rotate(proj[:, h * HEAD:(h + 1) * HEAD])
        q[h * ROWS:(h + 1) * ROWS, :] = (u * SCALE).astype(BF16)
    home[0, CHUNK:, :] = rotate(proj[:, 1024:1152]).astype(BF16)
    home[1, CHUNK:, :] = proj[:, 1152:1280].astype(BF16)

    for d in range(4, TP):
        a_copy(d).wait_recv()
    start("own_b_up", "own_b_down", "own_b_across", ("sibling", OWN))

    def attend(start, count, keys, values, near=None):
        rows = pl.ds(start, count)
        scores = lax.dot_general(
            q[rows, :], keys, (((1,), (1,)), ((), ())), preferred_element_type=F32
        )
        if near is not None:
            scores = jnp.where(near, scores, -1e30)
        peak = jnp.max(scores, axis=1, keepdims=True)
        if near is None:
            before = top[rows, :]
            peak = jnp.maximum(before, peak)
            fade = jnp.exp2(before - peak)
        else:
            peak = jnp.broadcast_to(peak, (count, 128))
        top[rows, :] = peak
        weights = jnp.concatenate(
            [jnp.exp2(scores[:, j:j + 128] - peak) for j in range(0, SPAN, 128)], axis=1
        ).astype(BF16)
        both = jnp.concatenate([values, jnp.ones_like(values)], axis=1)
        part = jnp.dot(weights, both, preferred_element_type=F32)
        if near is None:
            acc[rows, :] = acc[rows, :] * jnp.concatenate([fade, fade], axis=1) + part
        else:
            acc[rows, :] = part

    def absorb(block):
        for j in range(0, CHUNK, SPAN):
            for start in range(0, GROUP * ROWS, TILE):
                attend(start, TILE, block[0, j:j + SPAN, :], block[1, j:j + SPAN, :])

    causal = (
        lax.broadcasted_iota(jnp.int32, (ROWS, ROWS), 1)
        <= lax.broadcasted_iota(jnp.int32, (ROWS, ROWS), 0)
    )
    for h in range(GROUP):
        attend(h * ROWS, ROWS, home[0, CHUNK:, :], home[1, CHUNK:, :], causal)
    absorb(home)

    def step(i, _):
        @pl.when(i == 0)
        def _():
            arrived("own_a_across")
            start("across_a_up", "across_a_down")
            arrived("own_a_up", "own_a_down")
            start(("sibling", NEAR_A))
            arrived(("sibling", OWN))

        @pl.when(i == 1)
        def _():
            arrived("own_b_across")
            start(("sibling", ACROSS))
            arrived(("sibling", NEAR_A))

        @pl.when(i == 2)
        def _():
            arrived("own_b_up", "own_b_down")
            start("up_b_across", "down_b_across", "far_b", "far_a", ("sibling", NEAR_B))
            arrived(("sibling", ACROSS))

        @pl.when(i == 3)
        def _():
            arrived("across_a_up", "across_a_down")
            start("far_across_up", "far_across_down", ("sibling", ACROSS_A))
            arrived(("sibling", NEAR_B))

        @pl.when(i == 4)
        def _():
            arrived("far_b")
            start("far_b_across")
            arrived("far_a")
            start(("sibling", FAR))
            arrived(("sibling", ACROSS_A))

        @pl.when(i == 5)
        def _():
            arrived("up_b_across", "down_b_across")
            start(("sibling", ACROSS_B))
            arrived(("sibling", FAR))

        @pl.when(i == 6)
        def _():
            arrived("far_across_up", "far_across_down", "far_b_across")
            start(("sibling", FAR_ACROSS))
            arrived(("sibling", ACROSS_B))

        absorb(kv.at[2 * i])
        absorb(kv.at[2 * i + 1])
        return 0

    lax.fori_loop(0, 7, step, 0)

    arrived(("sibling", FAR_ACROSS))
    absorb(kv.at[14])
    for h in range(GROUP):
        rows = pl.ds(h * ROWS, ROWS)
        result = acc[rows, 0:HEAD] / acc[rows, HEAD:2 * HEAD]
        out[:, h * HEAD:(h + 1) * HEAD] = result.astype(BF16)

    for d in range(1, TP):
        a_copy(d).wait_send()
    for copy in moves.values():
        copy.wait_send()


def shards(tokens, norm_gain, query_weight, key_matrix, value_matrix, prompt_cache, lengths):
    cache = prompt_cache.reshape(2 * PIECE * TP, HEAD)
    gain = norm_gain.reshape(PARTS, 1, PART)
    cosine, sine = tables()
    hbm = pl.BlockSpec(memory_space=pl.ANY)
    vmem = pl.BlockSpec(memory_space=pltpu.VMEM)
    context = pl.pallas_call(
        kernel,
        out_shape=jax.ShapeDtypeStruct((ROWS, GROUP * HEAD), BF16),
        in_specs=[hbm] * 8,
        out_specs=vmem,
        scratch_shapes=[
            pltpu.VMEM((PARTS, 1, PART), F32),
            pltpu.VMEM((ROWS, HEAD), F32),
            pltpu.VMEM((ROWS, HEAD), F32),
            pltpu.VMEM((PARTS, ROWS, PART), BF16),
            pltpu.VMEM((PARTS, ROWS, PART), BF16),
            pltpu.VMEM((PARTS, PART, GROUP * HEAD), BF16),
            pltpu.VMEM((PARTS, PART, HEAD), BF16),
            pltpu.VMEM((PARTS, PART, HEAD), BF16),
            pltpu.VMEM((ROWS, (GROUP + 2) * HEAD), F32),
            pltpu.VMEM((2 * PIECE * TP, HEAD), BF16),
            pltpu.VMEM((2 * PIECE * TP, HEAD), F32),
            pltpu.VMEM((TP, 2, PIECE, HEAD), BF16),
            pltpu.VMEM((2, CHUNK + ROWS, HEAD), BF16),
            pltpu.VMEM((ROLLOUT - 1, 2, CHUNK, HEAD), BF16),
            pltpu.VMEM((GROUP * ROWS, HEAD), BF16),
            pltpu.VMEM((GROUP * ROWS, 128), F32),
            pltpu.VMEM((GROUP * ROWS, 2 * HEAD), F32),
            pltpu.SemaphoreType.DMA((3,)),
            pltpu.SemaphoreType.DMA((PARTS,)),
            pltpu.SemaphoreType.DMA((3, PARTS)),
            pltpu.SemaphoreType.DMA,
            pltpu.SemaphoreType.DMA((TP - 1,)),
            pltpu.SemaphoreType.DMA((TP - 1,)),
            pltpu.SemaphoreType.DMA((23,)),
            pltpu.SemaphoreType.DMA((23,)),
        ],
        compiler_params=pltpu.CompilerParams(
            collective_id=0, has_side_effects=True, vmem_limit_bytes=62 << 20
        ),
        cost_estimate=pl.CostEstimate(
            flops=23_000_000_000, bytes_accessed=30_000_000, transcendentals=34_000_000
        ),
    )(
        tokens, gain, query_weight, key_matrix, value_matrix, cache,
        jnp.asarray(cosine), jnp.asarray(sine),
    )
    live = jnp.arange(ROWS)[:, None] < lengths[0]
    return jnp.where(live, context, jnp.zeros_like(context))


def solution(mesh):
    placed = (
        P("rollout", None),
        P(),
        P(None, "tp"),
        P(None, "tp"),
        P(None, "tp"),
        P(None, ("rollout", "tp"), None, None),
        P("rollout"),
    )
    return jax.shard_map(
        shards, mesh=mesh, in_specs=placed, out_specs=P("rollout", "tp"), check_vma=False
    )
```
